32 devices in a mesh: row: 4 (over y, x), col: 8 (over z, core).
Axes of the slice: x: 2, y: 2, z: 4, core: 2. Of those that a mesh axis runs over, the one named last changes fastest.
Arguments:
- points: float32 [8, 4096], P(None, ('row', 'col')), may hold values from -6 to 6
- lengthscale: float32 [8], replicated, may hold values from 1.5 to 4
- signal_var: float32 [1], replicated, may hold values from 0.002 to 0.01
- noise_var: float32 [1], replicated, may hold values from 0.3 to 1.5
- solution: float32 [4, 4096], P(None, ('row', 'col')), may hold values from -6 to 6
- residual: float32 [4, 4096], P(None, ('row', 'col')), may hold values from -30 to 30, as said below
- direction: float32 [4, 4096], P(None, ('row', 'col')), may hold values from -6 to 6
Outputs:
- new_solution: float32 [4, 4096], P(None, ('row', 'col'))
- new_residual: float32 [4, 4096], P(None, ('row', 'col'))
- new_direction: float32 [4, 4096], P(None, ('row', 'col'))
The draws below stay inside these ranges and needn't reach their ends.
Inputs may be any that keep to these rules, and one draw needn't show every extreme that they name: residual values, real-valued.
All inputs are finite; a program needn't handle non-finite values.
Results may differ from the reference program's by a relative error of at most 0.00017.
Values sent between devices are 32-bit elements; how exact they have to be, the bound alone decides.
A program may use at most 128 MiB of HBM per device.

```python
import math
import jax
import jax.numpy as jnp
from jax import lax

DIM = 8
RHS = 4
NPTS = 4096


def draw_residual(key, part):
    key = jax.random.fold_in(key, 5)
    first, second = jax.random.split(key)
    spread = jnp.exp(jax.random.uniform(second, (RHS, NPTS), jnp.float32) * jnp.log(10.0))
    ramp = 1.0 + 2.0 * jnp.arange(NPTS, dtype=jnp.float32) / NPTS
    base = jnp.clip(jax.random.normal(first, (RHS, NPTS), jnp.float32), -4.0, 4.0)
    return base * spread * ramp[None, :] * 0.25


def level_of(own_key, shape, shards, smallest, largest):
    def one(position, shards_of):
        steps = jax.random.uniform(jax.random.fold_in(jax.random.fold_in(own_key, 6), position), (shards_of,), jnp.float32, smallest / len(shards), largest / len(shards))
        return jnp.repeat(jnp.exp(steps), shape[position] // shards_of).reshape((-1,) + (1,) * (len(shape) - position - 1))

    gain = one(*shards[0])
    for cut in shards[1:]:
        gain = gain * one(*cut)
    return gain


def bell_draw(own_key, extent, scale, reach, cuts=(), held_as=jnp.bfloat16):
    array = jax.random.normal(own_key, extent, jnp.float32) * scale
    if len(cuts) > 0:
        array = level_of(own_key, extent, cuts, -0.22, 0.18) * array
    return jnp.clip(array, min=-reach, max=reach).astype(held_as)


def setup_inputs(seed: int = 0) -> dict:
    streams_of = jax.random.split(jax.random.key(seed), 8)
    return {
        "points": bell_draw(streams_of[0], (DIM, NPTS), 1.0, 6.0, ((1, 32),), jnp.float32),
        "lengthscale": jnp.clip(jnp.exp(jax.random.uniform(streams_of[1], (DIM,), jnp.float32, math.log(1.5), math.log(4.0))), 1.5, 4.0),
        "signal_var": jnp.clip(jnp.exp(jax.random.uniform(streams_of[2], (1,), jnp.float32, math.log(0.002), math.log(0.01))), 0.002, 0.01),
        "noise_var": jnp.clip(jax.random.uniform(streams_of[3], (1,), jnp.float32, 0.3, 1.5), 0.3, 1.5),
        "solution": bell_draw(streams_of[4], (RHS, NPTS), 1.0, 6.0, ((1, 32),), jnp.float32),
        "residual": draw_residual(jax.random.fold_in(streams_of[7], 71), 0),
        "direction": bell_draw(streams_of[6], (RHS, NPTS), 1.0, 6.0, ((1, 32),), jnp.float32),
    }


def kernel_apply(row_pts, col_pts, col_dir, scale):
    rows = row_pts.shape[1]
    block = min(256, rows)
    blocks = row_pts.reshape(row_pts.shape[0], rows // block, block).transpose(1, 0, 2)

    def one_block(left):
        dist_sq = jnp.zeros((left.shape[1], col_pts.shape[1]), jnp.float32)
        for dim_idx in range(left.shape[0]):
            delta = left[dim_idx][:, None] - col_pts[dim_idx][None, :]
            dist_sq = dist_sq + delta * delta
        radius = jnp.sqrt(dist_sq)
        root_five = jnp.sqrt(jnp.float32(5.0))
        values = scale * (1.0 + root_five * radius + 5.0 / 3.0 * dist_sq) * jnp.exp(-root_five * radius)
        return jnp.einsum('rc,kc->kr', values, col_dir, precision=lax.Precision.HIGHEST)
    result = lax.map(one_block, blocks)
    return result.transpose(1, 0, 2).reshape(col_dir.shape[0], rows)

def reference(points, lengthscale, signal_var, noise_var, solution, residual, direction):
    scaled = points / lengthscale[:, None]
    image = kernel_apply(scaled, scaled, direction, signal_var[0]) + noise_var[0] * direction
    old_rr = lax.optimization_barrier(jnp.sum(residual * residual, axis=1))
    curv = lax.optimization_barrier(jnp.sum(direction * image, axis=1))
    alpha = old_rr / curv
    new_solution = solution + alpha[:, None] * direction
    new_residual = residual - alpha[:, None] * image
    new_rr = lax.optimization_barrier(jnp.sum(new_residual * new_residual, axis=1))
    new_direction = new_residual + (new_rr / old_rr)[:, None] * direction
    return (new_solution, new_residual, new_direction)
```

```python
import functools
import math

import jax
import jax.numpy as jnp
from jax import lax
from jax.experimental import pallas as pl
from jax.experimental.pallas import tpu as pltpu
from jax.sharding import PartitionSpec as P

MESH = pl.DeviceIdType.MESH
F32 = jnp.float32
BF16 = jnp.bfloat16
LN2 = math.log(2.0)
STEP = math.sqrt(5.0) / LN2
SLOTS = 4


def split3(x):
    a = x.astype(BF16).astype(F32)
    rest = x - a
    b = rest.astype(BF16).astype(F32)
    c = (rest - b).astype(BF16).astype(F32)
    return a, b, c


def norm_rows(x, first):
    n1, n2, n3 = split3(jnp.sum(x * x, axis=0, keepdims=True))
    row = lax.broadcasted_iota(jnp.int32, x.shape, 0)
    base = 0 if first else 3
    ones = (row >= 3 - base) & (row < 6 - base)
    out = jnp.where(ones, 1.0, 0.0)
    for i, part in enumerate((n1, n2, n3)):
        out = jnp.where(row == base + i, part, out)
    return out


def left_rows(x):
    a, b, c = split3(x)
    rows = [-2.0 * v for v in (a, a, b, b, a, c)]
    return jnp.concatenate(rows + [norm_rows(x, False), jnp.zeros_like(x)], axis=0)


def right_rows(x):
    a, b, c = split3(x)
    return jnp.concatenate([a, b, a, b, c, a, norm_rows(x, True), jnp.zeros_like(x)], axis=0)


def cg_kernel(rows, cols, len_ref, sig_ref, noise_ref, pts_ref, sol_ref, res_ref, dir_ref,
              nsol_ref, nres_ref, ndir_ref, held, sums, send_sem, recv_sem, sum_send, sum_recv):
    n = rows * cols
    me = lax.axis_index("row") * cols + lax.axis_index("col")
    dims, width = pts_ref.shape
    rhs = dir_ref.shape[0]

    def peer_of(k):
        peer = lax.rem(me + k, n)
        return (peer // cols, lax.rem(peer, cols))

    barrier = pltpu.get_barrier_semaphore()

    @pl.loop(1, n)
    def _(k):
        pl.semaphore_signal(barrier, inc=1, device_id=peer_of(k), device_id_type=MESH)

    held[me, :, 0:width] = pts_ref[0:rhs, :]
    held[me, :, width:2 * width] = pts_ref[rhs:dims, :]
    held[me, :, 2 * width:] = dir_ref[...]
    pl.semaphore_wait(barrier, n - 1)

    @pl.loop(1, n)
    def _(k):
        pltpu.make_async_remote_copy(
            src_ref=held.at[me], dst_ref=held.at[me], send_sem=send_sem, recv_sem=recv_sem,
            device_id=peer_of(k), device_id_type=MESH).start()

    row = lax.broadcasted_iota(jnp.int32, (dims, width), 0)
    scale = jnp.zeros((dims, width), F32)
    for i in range(dims):
        scale = jnp.where(row == i, len_ref[i], scale)
    scale = STEP / scale
    left = left_rows(pts_ref[...] * scale).T.astype(BF16)
    direction = dir_ref[...]
    residual = res_ref[...]

    pltpu.make_async_copy(held.at[pl.ds(0, n - 1)], held.at[pl.ds(0, n - 1)], recv_sem).wait()

    def chunk(c, total):
        right, dirs = [], []
        for j in range(SLOTS):
            block = held[c * SLOTS + j]
            x = jnp.concatenate([block[:, 0:width], block[:, width:2 * width]], axis=0)
            right.append(right_rows(x * scale))
            dirs.append(block[:, 2 * width:])
        right = jnp.concatenate(right, axis=1).astype(BF16)
        dirs = jnp.concatenate(dirs, axis=1)
        d1, d2, d3 = split3(dirs)
        dirs = jnp.concatenate([d1, d2, d3, jnp.zeros_like(d1)], axis=0).astype(BF16)
        v = jnp.maximum(jnp.dot(left, right, preferred_element_type=F32), 1e-30)
        w = v * lax.rsqrt(v)
        k = (1.0 + LN2 * w + (LN2 * LN2 / 3.0) * v) * jnp.exp2(-w)
        k1 = k.astype(BF16)
        k2 = (k - k1.astype(F32)).astype(BF16)
        nt = (((1,), (1,)), ((), ()))
        return (total + lax.dot_general(k1, dirs, nt, preferred_element_type=F32)
                + lax.dot_general(k2, dirs, nt, preferred_element_type=F32))

    total = lax.fori_loop(0, n // SLOTS, chunk, jnp.zeros((width, 4 * rhs), F32))
    total = total.T
    total = total[0:rhs] + total[rhs:2 * rhs] + total[2 * rhs:3 * rhs]
    image = sig_ref[0] * total + noise_ref[0] * direction

    def over(x):
        return jnp.sum(x, axis=1, keepdims=True)

    dq, rr, rq, qq = over(direction * image), over(residual * residual), over(residual * image), over(image * image)
    fits = qq > 1e-30
    near = jnp.where(fits, rq / jnp.where(fits, qq, 1.0), 0.0)
    left_over = residual - near * image
    pq, pp = over(left_over * image), over(left_over * left_over)
    lane = lax.broadcasted_iota(jnp.int32, (rhs, width), 1)
    sub = lax.broadcasted_iota(jnp.int32, (rhs, width), 0)
    mine = jnp.zeros((rhs, width), F32)
    for i, part in enumerate((dq, rr, near, qq, pq, pp)):
        mine = jnp.where(lane == sub + i * rhs, part, mine)
    sums[me] = jnp.sum(mine, axis=0, keepdims=True)

    @pl.loop(1, n)
    def _(k):
        pltpu.make_async_remote_copy(
            src_ref=sums.at[me], dst_ref=sums.at[me], send_sem=sum_send, recv_sem=sum_recv,
            device_id=peer_of(k), device_id_type=MESH).start()

    pltpu.make_async_copy(held.at[pl.ds(0, n - 1)], held.at[pl.ds(0, n - 1)], send_sem).wait()
    pltpu.make_async_copy(sums.at[pl.ds(0, n - 1)], sums.at[pl.ds(0, n - 1)], sum_recv).wait()

    every = sums[:, 0, :]

    def part(x, i):
        return x if i == 0 else pltpu.roll(x, width - i * rhs, 1)

    whole = jnp.sum(every, axis=0, keepdims=True)
    all_rr = jnp.sum(part(every, 1), axis=0, keepdims=True)
    used = lax.broadcasted_iota(jnp.int32, (1, width), 1) < rhs
    alpha = all_rr / jnp.where(used, whole, 1.0)
    off = alpha - part(every, 2)
    new_rr = jnp.sum(part(every, 5) + off * (off * part(every, 3) - 2.0 * part(every, 4)), axis=0, keepdims=True)
    beta = new_rr / jnp.where(used, all_rr, 1.0)
    diag = lane == sub
    alpha = over(jnp.where(diag, alpha, 0.0))
    beta = over(jnp.where(diag, beta, 0.0))
    nsol_ref[...] = sol_ref[...] + alpha * direction
    new_residual = residual - alpha * image
    nres_ref[...] = new_residual
    ndir_ref[...] = new_residual + beta * direction
    pltpu.make_async_copy(sums.at[pl.ds(0, n - 1)], sums.at[pl.ds(0, n - 1)], sum_send).wait()


def solution(mesh):
    rows, cols = mesh.shape["row"], mesh.shape["col"]
    n = rows * cols

    def on_device(points, lengthscale, signal_var, noise_var, solution, residual, direction):
        rhs, width = direction.shape
        vmem = pl.BlockSpec(memory_space=pltpu.VMEM)
        smem = pl.BlockSpec(memory_space=pltpu.SMEM)
        out = jax.ShapeDtypeStruct((rhs, width), F32)
        return pl.pallas_call(
            functools.partial(cg_kernel, rows, cols),
            out_shape=(out, out, out),
            in_specs=[smem] * 3 + [vmem] * 4,
            out_specs=(vmem, vmem, vmem),
            scratch_shapes=[
                pltpu.VMEM((n, rhs, 3 * width), F32),
                pltpu.VMEM((n, 1, width), F32),
                pltpu.SemaphoreType.DMA,
                pltpu.SemaphoreType.DMA,
                pltpu.SemaphoreType.DMA,
                pltpu.SemaphoreType.DMA,
            ],
            compiler_params=pltpu.CompilerParams(
                collective_id=0, has_side_effects=True, vmem_limit_bytes=32 * 1024 * 1024),
            cost_estimate=pl.CostEstimate(
                flops=2 * 80 * n * width * width, bytes_accessed=32 * 1024,
                transcendentals=2 * n * width * width),
        )(lengthscale, signal_var, noise_var, points, solution, residual, direction)

    spread = P(None, ("row", "col"))
    return jax.shard_map(
        on_device, mesh=mesh, in_specs=(spread, P(), P(), P(), spread, spread, spread),
        out_specs=(spread, spread, spread), check_vma=False)
```

```python
import functools
import math

import jax
import jax.numpy as jnp
from jax import lax
from jax.experimental import pallas as pl
from jax.experimental.pallas import tpu as pltpu
from jax.sharding import PartitionSpec as P

MESH = pl.DeviceIdType.MESH
F32 = jnp.float32
BF16 = jnp.bfloat16
LN2 = math.log(2.0)
STEP = math.sqrt(5.0) / LN2


def split3(x):
    a = x.astype(BF16).astype(F32)
    rest = x - a
    b = rest.astype(BF16).astype(F32)
    c = (rest - b).astype(BF16).astype(F32)
    return a, b, c


def norm_rows(x, first):
    n1, n2, n3 = split3(jnp.sum(x * x, axis=0, keepdims=True))
    row = lax.broadcasted_iota(jnp.int32, x.shape, 0)
    base = 0 if first else 3
    ones = (row >= 3 - base) & (row < 6 - base)
    out = jnp.where(ones, 1.0, 0.0)
    for i, part in enumerate((n1, n2, n3)):
        out = jnp.where(row == base + i, part, out)
    return out


def left_rows(x):
    a, b, c = split3(x)
    rows = [-2.0 * v for v in (a, a, b, b, a, c)]
    return jnp.concatenate(rows + [norm_rows(x, False), jnp.zeros_like(x)], axis=0)


def right_rows(x):
    a, b, c = split3(x)
    return jnp.concatenate([a, b, a, b, c, a, norm_rows(x, True), jnp.zeros_like(x)], axis=0)


def each(low, high, body):
    if high - low < 32:
        for k in range(low, high):
            body(k)
    else:
        pl.loop(low, high)(body)


def cg_kernel(rows, cols, len_hbm, sig_hbm, noise_hbm, pts_hbm, res_hbm, dir_hbm,
              move_ref,
              len_ref, sig_ref, noise_ref, res_ref, row_pts, col_all, made, got, sums, in_sem,
              pts_send, pts_recv, all_send, all_recv, part_send, part_recv, sum_send, sum_recv):
    n = rows * cols
    my_row, my_col = lax.axis_index("row"), lax.axis_index("col")
    me = my_row * cols + my_col
    _, dims, width = row_pts.shape
    rhs = res_ref.shape[0]

    def along(k):
        return lax.rem(my_col + k, cols)

    def across(k):
        return lax.rem(my_row + k, rows)

    def anyone(k):
        peer = lax.rem(me + k, n)
        return (peer // cols, lax.rem(peer, cols))

    mine_in = [
        pltpu.make_async_copy(pts_hbm, row_pts.at[my_col], in_sem.at[0]),
        pltpu.make_async_copy(dir_hbm, col_all.at[my_row, :, pl.ds(2 * width, width)], in_sem.at[1]),
        pltpu.make_async_copy(len_hbm, len_ref, in_sem.at[2]),
        pltpu.make_async_copy(res_hbm, res_ref, in_sem.at[3]),
        pltpu.make_async_copy(sig_hbm, sig_ref, in_sem.at[4]),
        pltpu.make_async_copy(noise_hbm, noise_ref, in_sem.at[5]),
    ]
    for copy in mine_in:
        copy.start()

    barrier = pltpu.get_barrier_semaphore()

    def greet(k):
        pl.semaphore_signal(barrier, inc=1, device_id=anyone(k), device_id_type=MESH)

    each(1, n, greet)
    mine_in[0].wait()
    mine_in[1].wait()
    points = row_pts[my_col]
    col_all[my_row, :, 0:width] = points[0:rhs]
    col_all[my_row, :, width:2 * width] = points[rhs:dims]
    pl.semaphore_wait(barrier, n - 1)

    def send_all(k):
        pltpu.make_async_remote_copy(
            src_ref=col_all.at[my_row], dst_ref=col_all.at[my_row], send_sem=all_send,
            recv_sem=all_recv, device_id=(across(k), my_col), device_id_type=MESH).start()

    def send_pts(k):
        pltpu.make_async_remote_copy(
            src_ref=row_pts.at[my_col], dst_ref=row_pts.at[my_col], send_sem=pts_send,
            recv_sem=pts_recv, device_id=(my_row, along(k)), device_id_type=MESH).start()

    each(1, rows, send_all)
    each(1, cols, send_pts)

    for copy in mine_in[2:]:
        copy.wait()
    row = lax.broadcasted_iota(jnp.int32, (dims, width), 0)
    scale = jnp.zeros((dims, width), F32)
    for i in range(dims):
        scale = jnp.where(row == i, len_ref[i], scale)
    scale = STEP / scale
    residual = res_ref[...]
    direction = col_all[my_row, :, 2 * width:]

    def wait_bytes(ref, count, sem):
        pltpu.make_async_copy(ref.at[pl.ds(0, count)], ref.at[pl.ds(0, count)], sem).wait()

    wait_bytes(col_all, rows - 1, all_recv)
    right, dirs = [], []
    for j in range(rows):
        block = col_all[j]
        x = jnp.concatenate([block[:, 0:width], block[:, width:2 * width]], axis=0)
        right.append(right_rows(x * scale))
        dirs.append(block[:, 2 * width:])
    right = jnp.concatenate(right, axis=1).astype(BF16)
    d1, d2, d3 = split3(jnp.concatenate(dirs, axis=1))
    dirs = jnp.concatenate([d1, d2, d3, jnp.zeros_like(d1)], axis=0).astype(BF16)
    wait_bytes(row_pts, cols - 1, pts_recv)

    def slab(k):
        to = along(k)
        left = left_rows(row_pts[to] * scale).T.astype(BF16)
        v = jnp.maximum(jnp.dot(left, right, preferred_element_type=F32), 1e-30)
        w = v * lax.rsqrt(v)
        kern = (1.0 + LN2 * w + (LN2 * LN2 / 3.0) * v) * jnp.exp2(-w)
        k1 = kern.astype(BF16)
        k2 = (kern - k1.astype(F32)).astype(BF16)
        nt = (((1,), (1,)), ((), ()))
        total = (lax.dot_general(k1, dirs, nt, preferred_element_type=F32)
                 + lax.dot_general(k2, dirs, nt, preferred_element_type=F32)).T
        return to, total[0:rhs] + total[rhs:2 * rhs] + total[2 * rhs:3 * rhs]

    def send_part(k):
        to, total = slab(k)
        made[to] = total
        pltpu.make_async_remote_copy(
            src_ref=made.at[to], dst_ref=got.at[my_col], send_sem=part_send, recv_sem=part_recv,
            device_id=(my_row, to), device_id_type=MESH).start()

    each(1, cols, send_part)
    got[my_col] = slab(0)[1]
    wait_bytes(got, cols - 1, part_recv)
    image = sig_ref[0, 0] * jnp.sum(got[...], axis=0) + noise_ref[0, 0] * direction

    def over(x):
        return jnp.sum(x, axis=1, keepdims=True)

    dq, rr, rq, qq = over(direction * image), over(residual * residual), over(residual * image), over(image * image)
    fits = qq > 1e-30
    near = jnp.where(fits, rq / jnp.where(fits, qq, 1.0), 0.0)
    left_over = residual - near * image
    pq, pp = over(left_over * image), over(left_over * left_over)
    lane = lax.broadcasted_iota(jnp.int32, (rhs, width), 1)
    sub = lax.broadcasted_iota(jnp.int32, (rhs, width), 0)
    mine = jnp.zeros((rhs, width), F32)
    for i, part in enumerate((dq, rr, near, qq, pq, pp)):
        mine = jnp.where(lane == sub + i * rhs, part, mine)
    sums[me] = jnp.sum(mine, axis=0, keepdims=True)

    def send_sum(k):
        pltpu.make_async_remote_copy(
            src_ref=sums.at[me], dst_ref=sums.at[me], send_sem=sum_send, recv_sem=sum_recv,
            device_id=anyone(k), device_id_type=MESH).start()

    each(1, n, send_sum)
    wait_bytes(col_all, rows - 1, all_send)
    wait_bytes(row_pts, cols - 1, pts_send)
    wait_bytes(made, cols - 1, part_send)
    wait_bytes(sums, n - 1, sum_recv)

    every = sums[:, 0, :]

    def part(x, i):
        return x if i == 0 else pltpu.roll(x, width - i * rhs, 1)

    whole = jnp.sum(every, axis=0, keepdims=True)
    all_rr = jnp.sum(part(every, 1), axis=0, keepdims=True)
    used = lax.broadcasted_iota(jnp.int32, (1, width), 1) < rhs
    alpha = all_rr / jnp.where(used, whole, 1.0)
    off = alpha - part(every, 2)
    new_rr = jnp.sum(part(every, 5) + off * (off * part(every, 3) - 2.0 * part(every, 4)), axis=0, keepdims=True)
    beta = new_rr / jnp.where(used, all_rr, 1.0)
    diag = lane == sub
    alpha = over(jnp.where(diag, alpha, 0.0))
    beta = over(jnp.where(diag, beta, 0.0))
    move_ref[0] = alpha * direction
    move_ref[1] = alpha * image
    move_ref[2] = beta * direction
    wait_bytes(sums, n - 1, sum_send)


def solution(mesh):
    rows, cols = mesh.shape["row"], mesh.shape["col"]
    n = rows * cols

    def on_device(points, lengthscale, signal_var, noise_var, solution, residual, direction):
        rhs, width = direction.shape
        dims = points.shape[0]
        vmem = pl.BlockSpec(memory_space=pltpu.VMEM)
        hbm = pl.BlockSpec(memory_space=pltpu.HBM)
        move = pl.pallas_call(
            functools.partial(cg_kernel, rows, cols),
            out_shape=jax.ShapeDtypeStruct((3, rhs, width), F32),
            in_specs=[hbm] * 6,
            out_specs=vmem,
            scratch_shapes=[
                pltpu.SMEM((dims,), F32),
                pltpu.SMEM((1, 1), F32),
                pltpu.SMEM((1, 1), F32),
                pltpu.VMEM((rhs, width), F32),
                pltpu.VMEM((cols, dims, width), F32),
                pltpu.VMEM((rows, rhs, 3 * width), F32),
                pltpu.VMEM((cols, rhs, width), F32),
                pltpu.VMEM((cols, rhs, width), F32),
                pltpu.VMEM((n, 1, width), F32),
                pltpu.SemaphoreType.DMA((6,)),
            ] + [pltpu.SemaphoreType.DMA] * 8,
            compiler_params=pltpu.CompilerParams(
                collective_id=0, has_side_effects=True, vmem_limit_bytes=60 * 1024 * 1024),
            cost_estimate=pl.CostEstimate(
                flops=2 * 80 * n * width * width, bytes_accessed=32 * 1024,
                transcendentals=2 * n * width * width),
        )(lengthscale, signal_var.reshape(1, 1), noise_var.reshape(1, 1), points, residual, direction)
        new_residual = residual - move[1]
        return solution + move[0], new_residual, new_residual + move[2]

    spread = P(None, ("row", "col"))
    return jax.shard_map(
        on_device, mesh=mesh, in_specs=(spread, P(), P(), P(), spread, spread, spread),
        out_specs=(spread, spread, spread), check_vma=False)
```

```python
import functools
import math

import jax
import jax.numpy as jnp
from jax import lax
from jax.experimental import pallas as pl
from jax.experimental.pallas import tpu as pltpu
from jax.sharding import PartitionSpec as P

MESH = pl.DeviceIdType.MESH
F32 = jnp.float32
BF16 = jnp.bfloat16
LN2 = math.log(2.0)
STEP = math.sqrt(5.0) / LN2


def split3(x):
    a = x.astype(BF16).astype(F32)
    rest = x - a
    b = rest.astype(BF16).astype(F32)
    c = (rest - b).astype(BF16).astype(F32)
    return a, b, c


def norm_rows(x, first):
    n1, n2, n3 = split3(jnp.sum(x * x, axis=0, keepdims=True))
    row = lax.broadcasted_iota(jnp.int32, x.shape, 0)
    base = 0 if first else 3
    ones = (row >= 3 - base) & (row < 6 - base)
    out = jnp.where(ones, 1.0, 0.0)
    for i, part in enumerate((n1, n2, n3)):
        out = jnp.where(row == base + i, part, out)
    return out


def left_rows(x):
    a, b, c = split3(x)
    rows = [-2.0 * v for v in (a, a, b, b, a, c)]
    return jnp.concatenate(rows + [norm_rows(x, False), jnp.zeros_like(x)], axis=0)


def right_rows(x):
    a, b, c = split3(x)
    return jnp.concatenate([a, b, a, b, c, a, norm_rows(x, True), jnp.zeros_like(x)], axis=0)


def each(low, high, body):
    for k in range(low, high):
        body(k)


def block_of(left, right, dirs):
    rhs = dirs.shape[0] // 4
    v = jnp.maximum(jnp.dot(left, right, preferred_element_type=F32), 1e-30)
    w = v * lax.rsqrt(v)
    kern = (1.0 + LN2 * w + (LN2 * LN2 / 3.0) * v) * jnp.exp2(-w)
    k1 = kern.astype(BF16)
    k2 = (kern - k1.astype(F32)).astype(BF16)
    total = jnp.dot(dirs, k1, preferred_element_type=F32) + jnp.dot(dirs, k2, preferred_element_type=F32)
    return total[0:rhs] + total[rhs:2 * rhs] + total[2 * rhs:3 * rhs]


def cg_kernel(rows, cols, len_hbm, sig_hbm, noise_hbm, pts_hbm, res_hbm, dir_hbm, move_ref,
              len_ref, sig_ref, noise_ref, pts_ref, res_ref, dir_ref, row_all, col_all, parts, images, sums, in_sem,
              row_send, row_recv, col_send, col_recv, part_send, part_recv, sum_send, sum_recv):
    my_row, my_col = lax.axis_index("row"), lax.axis_index("col")
    dims, width = pts_ref.shape
    rhs = res_ref.shape[0]

    def along(k):
        return (my_row, lax.rem(my_col + k, cols))

    def across(k):
        return (lax.rem(my_row + k, rows), my_col)

    mine_in = [
        pltpu.make_async_copy(pts_hbm, pts_ref, in_sem.at[0]),
        pltpu.make_async_copy(dir_hbm, dir_ref, in_sem.at[1]),
        pltpu.make_async_copy(res_hbm, res_ref, in_sem.at[2]),
        pltpu.make_async_copy(len_hbm, len_ref, in_sem.at[3]),
        pltpu.make_async_copy(sig_hbm, sig_ref, in_sem.at[4]),
        pltpu.make_async_copy(noise_hbm, noise_ref, in_sem.at[5]),
    ]
    for copy in mine_in:
        copy.start()

    barrier = pltpu.get_barrier_semaphore()
    each(1, cols, lambda k: pl.semaphore_signal(
        barrier, inc=1, device_id=along(k), device_id_type=MESH))
    each(1, rows, lambda k: pl.semaphore_signal(
        barrier, inc=1, device_id=across(k), device_id_type=MESH))
    for copy in mine_in[0:3]:
        copy.wait()
    row_all[my_col, :, 0:width] = pts_ref[0:rhs]
    row_all[my_col, :, width:2 * width] = pts_ref[rhs:dims]
    row_all[my_col, :, 2 * width:] = dir_ref[...]
    col_all[my_row, :, 0:width] = pts_ref[0:rhs]
    col_all[my_row, :, width:2 * width] = pts_ref[rhs:dims]
    col_all[my_row, :, 2 * width:3 * width] = dir_ref[...]
    col_all[my_row, :, 3 * width:] = res_ref[...]
    pl.semaphore_wait(barrier, cols - 1 + rows - 1)

    def share(ref, slot, send_sem, recv_sem, peer):
        pltpu.make_async_remote_copy(
            src_ref=ref.at[slot], dst_ref=ref.at[slot], send_sem=send_sem, recv_sem=recv_sem,
            device_id=peer, device_id_type=MESH).start()

    def wait_bytes(ref, sem):
        count = ref.shape[0] - 1
        pltpu.make_async_copy(ref.at[pl.ds(0, count)], ref.at[pl.ds(0, count)], sem).wait()

    each(1, cols, lambda k: share(row_all, my_col, row_send, row_recv, along(k)))
    each(1, rows, lambda k: share(col_all, my_row, col_send, col_recv, across(k)))

    for copy in mine_in[3:]:
        copy.wait()
    row = lax.broadcasted_iota(jnp.int32, (dims, width), 0)
    scale = jnp.zeros((dims, width), F32)
    for i in range(dims):
        scale = jnp.where(row == i, len_ref[i], scale)
    scale = STEP / scale

    def points_of(block):
        return jnp.concatenate([block[:, 0:width], block[:, width:2 * width]], axis=0) * scale

    wait_bytes(col_all, col_recv)
    right = jnp.concatenate([right_rows(points_of(col_all[j])) for j in range(rows)], axis=1).astype(BF16)
    wait_bytes(row_all, row_recv)

    def from_slots(first):
        left, dirs = [], []
        for j in range(group):
            block = row_all[first + j]
            left.append(left_rows(points_of(block)))
            dirs.append(block[:, 2 * width:3 * width])
        left = jnp.concatenate(left, axis=1).T.astype(BF16)
        d1, d2, d3 = split3(jnp.concatenate(dirs, axis=1))
        dirs = jnp.concatenate([d1, d2, d3, jnp.zeros_like(d1)], axis=0).astype(BF16)
        return block_of(left, right, dirs)

    group = math.gcd(cols, max(1, 8 * 4 // rows))
    if group == cols:
        part = from_slots(0)
    else:
        part = lax.fori_loop(0, cols // group, lambda c, acc: acc + from_slots(c * group),
                             jnp.zeros((rhs, rows * width), F32))
    parts[my_row] = part
    each(1, rows, lambda k: share(parts, my_row, part_send, part_recv, across(k)))

    direction = jnp.concatenate([col_all[j, :, 2 * width:3 * width] for j in range(rows)], axis=1)
    residual = jnp.concatenate([col_all[j, :, 3 * width:] for j in range(rows)], axis=1)
    wait_bytes(parts, part_recv)
    image = sig_ref[0, 0] * jnp.sum(parts[...], axis=0) + noise_ref[0, 0] * direction

    def over(x):
        return jnp.sum(x, axis=1, keepdims=True)

    dq, rr, rq, qq = over(direction * image), over(residual * residual), over(residual * image), over(image * image)
    fits = qq > 1e-30
    near = jnp.where(fits, rq / jnp.where(fits, qq, 1.0), 0.0)
    left_over = residual - near * image
    pq, pp = over(left_over * image), over(left_over * left_over)
    lane = lax.broadcasted_iota(jnp.int32, (rhs, width), 1)
    sub = lax.broadcasted_iota(jnp.int32, (rhs, width), 0)
    mine = jnp.zeros((rhs, width), F32)
    for i, item in enumerate((dq, rr, near, qq, pq, pp)):
        mine = jnp.where(lane == sub + i * rhs, item, mine)
    sums[my_col] = jnp.sum(mine, axis=0, keepdims=True)
    each(1, cols, lambda k: share(sums, my_col, sum_send, sum_recv, along(k)))

    for j in range(rows):
        images[j] = image[:, j * width:(j + 1) * width]
    wait_bytes(row_all, row_send)
    wait_bytes(col_all, col_send)
    wait_bytes(parts, part_send)
    wait_bytes(sums, sum_recv)

    every = sums[:, 0, :]

    def item(i):
        return every if i == 0 else pltpu.roll(every, width - i * rhs, 1)

    whole = jnp.sum(every, axis=0, keepdims=True)
    all_rr = jnp.sum(item(1), axis=0, keepdims=True)
    used = lax.broadcasted_iota(jnp.int32, (1, width), 1) < rhs
    alpha = all_rr / jnp.where(used, whole, 1.0)
    off = alpha - item(2)
    new_rr = jnp.sum(item(5) + off * (off * item(3) - 2.0 * item(4)), axis=0, keepdims=True)
    beta = new_rr / jnp.where(used, all_rr, 1.0)
    diag = lane == sub
    alpha = over(jnp.where(diag, alpha, 0.0))
    beta = over(jnp.where(diag, beta, 0.0))
    move_ref[0] = alpha * dir_ref[...]
    move_ref[1] = alpha * images[my_row]
    move_ref[2] = beta * dir_ref[...]
    wait_bytes(sums, sum_send)


def solution(mesh):
    rows, cols = mesh.shape["row"], mesh.shape["col"]

    def on_device(points, lengthscale, signal_var, noise_var, solution, residual, direction):
        rhs, width = direction.shape
        dims = points.shape[0]
        vmem = pl.BlockSpec(memory_space=pltpu.VMEM)
        hbm = pl.BlockSpec(memory_space=pltpu.HBM)
        move = pl.pallas_call(
            functools.partial(cg_kernel, rows, cols),
            out_shape=jax.ShapeDtypeStruct((3, rhs, width), F32),
            in_specs=[hbm] * 6,
            out_specs=vmem,
            scratch_shapes=[
                pltpu.SMEM((dims,), F32),
                pltpu.SMEM((1, 1), F32),
                pltpu.SMEM((1, 1), F32),
                pltpu.VMEM((dims, width), F32),
                pltpu.VMEM((rhs, width), F32),
                pltpu.VMEM((rhs, width), F32),
                pltpu.VMEM((cols, rhs, 3 * width), F32),
                pltpu.VMEM((rows, rhs, 4 * width), F32),
                pltpu.VMEM((rows, rhs, rows * width), F32),
                pltpu.VMEM((rows, rhs, width), F32),
                pltpu.VMEM((cols, 1, width), F32),
                pltpu.SemaphoreType.DMA((6,)),
            ] + [pltpu.SemaphoreType.DMA] * 8,
            compiler_params=pltpu.CompilerParams(
                collective_id=0, has_side_effects=True, vmem_limit_bytes=60 * 1024 * 1024),
            cost_estimate=pl.CostEstimate(
                flops=2 * 80 * rows * cols * width * width, bytes_accessed=32 * 1024,
                transcendentals=2 * rows * cols * width * width),
        )(lengthscale, signal_var.reshape(1, 1), noise_var.reshape(1, 1), points, residual, direction)
        new_residual = residual - move[1]
        return solution + move[0], new_residual, new_residual + move[2]

    spread = P(None, ("row", "col"))
    return jax.shard_map(
        on_device, mesh=mesh, in_specs=(spread, P(), P(), P(), spread, spread, spread),
        out_specs=(spread, spread, spread), check_vma=False)
```

```python
import functools
import math

import jax
import jax.numpy as jnp
from jax import lax
from jax.experimental import pallas as pl
from jax.experimental.pallas import tpu as pltpu
from jax.sharding import PartitionSpec as P

MESH = pl.DeviceIdType.MESH
F32 = jnp.float32
BF16 = jnp.bfloat16
STEP = math.sqrt(5.0)
TILE = 256


def split3(x):
    a = x.astype(BF16).astype(F32)
    rest = x - a
    b = rest.astype(BF16).astype(F32)
    c = (rest - b).astype(BF16).astype(F32)
    return a, b, c


def norm_rows(x, first):
    n1, n2, n3 = split3(jnp.sum(x * x, axis=0, keepdims=True))
    row = lax.broadcasted_iota(jnp.int32, x.shape, 0)
    base = 0 if first else 3
    ones = (row >= 3 - base) & (row < 6 - base)
    out = jnp.where(ones, 1.0, 0.0)
    for i, part in enumerate((n1, n2, n3)):
        out = jnp.where(row == base + i, part, out)
    return out


def left_rows(x):
    a, b, c = split3(x)
    rows = [-2.0 * v for v in (a, a, b, b, a, c)]
    return jnp.concatenate(rows + [norm_rows(x, False), jnp.zeros_like(x)], axis=0)


def right_rows(x):
    a, b, c = split3(x)
    return jnp.concatenate([a, b, a, b, c, a, norm_rows(x, True), jnp.zeros_like(x)], axis=0)


def each(low, high, body):
    for k in range(low, high):
        body(k)


def block_of(left, right, dirs):
    rhs = dirs.shape[0] // 4
    deep, wide = min(128, left.shape[0]), min(TILE, right.shape[1])
    out = []
    for j in range(0, right.shape[1], wide):
        total = jnp.zeros((dirs.shape[0], wide), F32)
        for i in range(0, left.shape[0], deep):
            v = jnp.dot(left[i:i + deep], right[:, j:j + wide], preferred_element_type=F32)
            v = jnp.maximum(v, 1e-30)
            t = v * lax.rsqrt(v)
            kern = (1.0 + t + (1.0 / 3.0) * v) * jnp.exp(-t)
            k1 = kern.astype(BF16)
            k2 = (kern - k1.astype(F32)).astype(BF16)
            rows = dirs[:, i:i + deep]
            total += jnp.dot(rows, k1, preferred_element_type=F32)
            total += jnp.dot(rows, k2, preferred_element_type=F32)
        out.append(total[0:rhs] + total[rhs:2 * rhs] + total[2 * rhs:3 * rhs])
    return jnp.concatenate(out, axis=1)


def cg_kernel(rows, cols, len_hbm, sig_hbm, noise_hbm, pts_hbm, res_hbm, dir_hbm, move_ref,
              len_ref, sig_ref, noise_ref, pts_ref, res_ref, dir_ref, row_all, col_all, parts, images, sums, in_sem,
              row_send, row_recv, col_send, col_recv, part_send, part_recv, sum_send, sum_recv):
    my_row, my_col = lax.axis_index("row"), lax.axis_index("col")
    dims, width = pts_ref.shape
    rhs = res_ref.shape[0]

    def along(k):
        return (my_row, lax.rem(my_col + k, cols))

    def across(k):
        return (lax.rem(my_row + k, rows), my_col)

    mine_in = [
        pltpu.make_async_copy(pts_hbm, pts_ref, in_sem.at[0]),
        pltpu.make_async_copy(dir_hbm, dir_ref, in_sem.at[1]),
        pltpu.make_async_copy(res_hbm, res_ref, in_sem.at[2]),
        pltpu.make_async_copy(len_hbm, len_ref, in_sem.at[3]),
        pltpu.make_async_copy(sig_hbm, sig_ref, in_sem.at[4]),
        pltpu.make_async_copy(noise_hbm, noise_ref, in_sem.at[5]),
    ]
    for copy in mine_in:
        copy.start()

    barrier = pltpu.get_barrier_semaphore()
    each(1, cols, lambda k: pl.semaphore_signal(
        barrier, inc=1, device_id=along(k), device_id_type=MESH))
    each(1, rows, lambda k: pl.semaphore_signal(
        barrier, inc=1, device_id=across(k), device_id_type=MESH))
    for copy in mine_in[0:3]:
        copy.wait()
    row_all[my_col, :, 0:width] = pts_ref[0:rhs]
    row_all[my_col, :, width:2 * width] = pts_ref[rhs:dims]
    row_all[my_col, :, 2 * width:] = dir_ref[...]
    col_all[my_row, :, 0:width] = pts_ref[0:rhs]
    col_all[my_row, :, width:2 * width] = pts_ref[rhs:dims]
    col_all[my_row, :, 2 * width:3 * width] = dir_ref[...]
    col_all[my_row, :, 3 * width:] = res_ref[...]
    pl.semaphore_wait(barrier, cols - 1 + rows - 1)

    def share(ref, slot, send_sem, recv_sem, peer):
        pltpu.make_async_remote_copy(
            src_ref=ref.at[slot], dst_ref=ref.at[slot], send_sem=send_sem, recv_sem=recv_sem,
            device_id=peer, device_id_type=MESH).start()

    def wait_bytes(ref, sem):
        count = ref.shape[0] - 1
        pltpu.make_async_copy(ref.at[pl.ds(0, count)], ref.at[pl.ds(0, count)], sem).wait()

    each(1, cols, lambda k: share(row_all, my_col, row_send, row_recv, along(k)))
    each(1, rows, lambda k: share(col_all, my_row, col_send, col_recv, across(k)))

    for copy in mine_in[3:]:
        copy.wait()
    row = lax.broadcasted_iota(jnp.int32, (dims, width), 0)
    scale = jnp.zeros((dims, width), F32)
    for i in range(dims):
        scale = jnp.where(row == i, len_ref[i], scale)
    scale = STEP / scale

    def points_of(block):
        return jnp.concatenate([block[:, 0:width], block[:, width:2 * width]], axis=0) * scale

    wait_bytes(col_all, col_recv)
    right = jnp.concatenate([right_rows(points_of(col_all[j])) for j in range(rows)], axis=1).astype(BF16)
    wait_bytes(row_all, row_recv)

    def from_slots(first):
        left, dirs = [], []
        for j in range(group):
            block = row_all[first + j]
            left.append(left_rows(points_of(block)))
            dirs.append(block[:, 2 * width:3 * width])
        left = jnp.concatenate(left, axis=1).T.astype(BF16)
        d1, d2, d3 = split3(jnp.concatenate(dirs, axis=1))
        dirs = jnp.concatenate([d1, d2, d3, jnp.zeros_like(d1)], axis=0).astype(BF16)
        return block_of(left, right, dirs)

    group = math.gcd(cols, max(1, 8 * 4 // rows))
    if group == cols:
        part = from_slots(0)
    else:
        part = lax.fori_loop(0, cols // group, lambda c, acc: acc + from_slots(c * group),
                             jnp.zeros((rhs, rows * width), F32))
    parts[my_row] = part
    each(1, rows, lambda k: share(parts, my_row, part_send, part_recv, across(k)))

    direction = jnp.concatenate([col_all[j, :, 2 * width:3 * width] for j in range(rows)], axis=1)
    residual = jnp.concatenate([col_all[j, :, 3 * width:] for j in range(rows)], axis=1)
    wait_bytes(parts, part_recv)
    image = sig_ref[0, 0] * jnp.sum(parts[...], axis=0) + noise_ref[0, 0] * direction

    def over(x):
        return jnp.sum(x, axis=1, keepdims=True)

    dq, rr, rq, qq = over(direction * image), over(residual * residual), over(residual * image), over(image * image)
    fits = qq > 1e-30
    near = jnp.where(fits, rq / jnp.where(fits, qq, 1.0), 0.0)
    left_over = residual - near * image
    pq, pp = over(left_over * image), over(left_over * left_over)
    lane = lax.broadcasted_iota(jnp.int32, (rhs, width), 1)
    sub = lax.broadcasted_iota(jnp.int32, (rhs, width), 0)
    mine = jnp.zeros((rhs, width), F32)
    for i, item in enumerate((dq, rr, near, qq, pq, pp)):
        mine = jnp.where(lane == sub + i * rhs, item, mine)
    sums[my_col] = jnp.sum(mine, axis=0, keepdims=True)
    each(1, cols, lambda k: share(sums, my_col, sum_send, sum_recv, along(k)))

    for j in range(rows):
        images[j] = image[:, j * width:(j + 1) * width]
    wait_bytes(row_all, row_send)
    wait_bytes(col_all, col_send)
    wait_bytes(parts, part_send)
    wait_bytes(sums, sum_recv)

    every = sums[:, 0, :]

    def item(i):
        return every if i == 0 else pltpu.roll(every, width - i * rhs, 1)

    whole = jnp.sum(every, axis=0, keepdims=True)
    all_rr = jnp.sum(item(1), axis=0, keepdims=True)
    used = lax.broadcasted_iota(jnp.int32, (1, width), 1) < rhs
    alpha = all_rr / jnp.where(used, whole, 1.0)
    off = alpha - item(2)
    new_rr = jnp.sum(item(5) + off * (off * item(3) - 2.0 * item(4)), axis=0, keepdims=True)
    beta = new_rr / jnp.where(used, all_rr, 1.0)
    diag = lane == sub
    alpha = over(jnp.where(diag, alpha, 0.0))
    beta = over(jnp.where(diag, beta, 0.0))
    move_ref[0] = alpha * dir_ref[...]
    move_ref[1] = alpha * images[my_row]
    move_ref[2] = beta * dir_ref[...]
    wait_bytes(sums, sum_send)


def solution(mesh):
    rows, cols = mesh.shape["row"], mesh.shape["col"]

    def on_device(points, lengthscale, signal_var, noise_var, solution, residual, direction):
        rhs, width = direction.shape
        dims = points.shape[0]
        vmem = pl.BlockSpec(memory_space=pltpu.VMEM)
        hbm = pl.BlockSpec(memory_space=pltpu.HBM)
        move = pl.pallas_call(
            functools.partial(cg_kernel, rows, cols),
            out_shape=jax.ShapeDtypeStruct((3, rhs, width), F32),
            in_specs=[hbm] * 6,
            out_specs=vmem,
            scratch_shapes=[
                pltpu.SMEM((dims,), F32),
                pltpu.SMEM((1, 1), F32),
                pltpu.SMEM((1, 1), F32),
                pltpu.VMEM((dims, width), F32),
                pltpu.VMEM((rhs, width), F32),
                pltpu.VMEM((rhs, width), F32),
                pltpu.VMEM((cols, rhs, 3 * width), F32),
                pltpu.VMEM((rows, rhs, 4 * width), F32),
                pltpu.VMEM((rows, rhs, rows * width), F32),
                pltpu.VMEM((rows, rhs, width), F32),
                pltpu.VMEM((cols, 1, width), F32),
                pltpu.SemaphoreType.DMA((6,)),
            ] + [pltpu.SemaphoreType.DMA] * 8,
            compiler_params=pltpu.CompilerParams(
                collective_id=0, has_side_effects=True, vmem_limit_bytes=60 * 1024 * 1024),
            cost_estimate=pl.CostEstimate(
                flops=2 * 80 * rows * cols * width * width, bytes_accessed=32 * 1024,
                transcendentals=2 * rows * cols * width * width),
        )(lengthscale, signal_var.reshape(1, 1), noise_var.reshape(1, 1), points, residual, direction)
        new_residual = residual - move[1]
        return solution + move[0], new_residual, new_residual + move[2]

    spread = P(None, ("row", "col"))
    return jax.shard_map(
        on_device, mesh=mesh, in_specs=(spread, P(), P(), P(), spread, spread, spread),
        out_specs=(spread, spread, spread), check_vma=False)
```

```python
import functools
import math

import jax
import jax.numpy as jnp
from jax import lax
from jax.experimental import pallas as pl
from jax.experimental.pallas import tpu as pltpu
from jax.sharding import PartitionSpec as P

MESH = pl.DeviceIdType.MESH
F32 = jnp.float32
BF16 = jnp.bfloat16
STEP = math.sqrt(5.0)
TILE = 256


def split3(x):
    a = x.astype(BF16).astype(F32)
    rest = x - a
    b = rest.astype(BF16).astype(F32)
    c = (rest - b).astype(BF16).astype(F32)
    return a, b, c


def norm_rows(x, first):
    n1, n2, n3 = split3(jnp.sum(x * x, axis=0, keepdims=True))
    row = lax.broadcasted_iota(jnp.int32, x.shape, 0)
    base = 0 if first else 3
    ones = (row >= 3 - base) & (row < 6 - base)
    out = jnp.where(ones, 1.0, 0.0)
    for i, part in enumerate((n1, n2, n3)):
        out = jnp.where(row == base + i, part, out)
    return out


def left_rows(x):
    a, b, c = split3(x)
    rows = [-2.0 * v for v in (a, a, b, b, a, c)]
    return jnp.concatenate(rows + [norm_rows(x, False), jnp.zeros_like(x)], axis=0)


def right_rows(x):
    a, b, c = split3(x)
    return jnp.concatenate([a, b, a, b, c, a, norm_rows(x, True), jnp.zeros_like(x)], axis=0)


def each(low, high, body):
    for k in range(low, high):
        body(k)


def add_block(totals, left, right, dirs):
    deep, wide = min(128, left.shape[0]), right.shape[1] // len(totals)
    out = []
    for j, total in enumerate(totals):
        for i in range(0, left.shape[0], deep):
            v = jnp.dot(left[i:i + deep], right[:, j * wide:(j + 1) * wide], preferred_element_type=F32)
            v = jnp.maximum(v, 1e-30)
            t = v * lax.rsqrt(v)
            kern = (1.0 + t + (1.0 / 3.0) * v) * jnp.exp(-t)
            k1 = kern.astype(BF16)
            k2 = (kern - k1.astype(F32)).astype(BF16)
            rows = dirs[:, i:i + deep]
            total += jnp.dot(rows, k1, preferred_element_type=F32)
            total += jnp.dot(rows, k2, preferred_element_type=F32)
        out.append(total)
    return out


def cg_kernel(rows, cols, len_hbm, sig_hbm, noise_hbm, pts_hbm, res_hbm, dir_hbm, move_ref,
              len_ref, sig_ref, noise_ref, pts_ref, res_ref, dir_ref, row_all, col_all, parts, images, sums, in_sem,
              row_send, row_recv, col_send, col_recv, part_send, part_recv, sum_send, sum_recv):
    my_row, my_col = lax.axis_index("row"), lax.axis_index("col")
    dims, width = pts_ref.shape
    rhs = res_ref.shape[0]

    def partner(k):
        if cols & (cols - 1):
            return lax.rem(my_col + k, cols), lax.rem(my_col + cols - k, cols)
        peer = my_col
        for b in range(cols.bit_length()):
            if (k >> b) & 1:
                peer = peer + (1 << b) - (2 << b) * lax.rem(my_col // (1 << b), 2)
        return peer, peer

    def along(k):
        return (my_row, partner(k)[0])

    def across(k):
        return (lax.rem(my_row + k, rows), my_col)

    mine_in = [
        pltpu.make_async_copy(pts_hbm, pts_ref, in_sem.at[0]),
        pltpu.make_async_copy(dir_hbm, dir_ref, in_sem.at[1]),
        pltpu.make_async_copy(res_hbm, res_ref, in_sem.at[2]),
        pltpu.make_async_copy(len_hbm, len_ref, in_sem.at[3]),
        pltpu.make_async_copy(sig_hbm, sig_ref, in_sem.at[4]),
        pltpu.make_async_copy(noise_hbm, noise_ref, in_sem.at[5]),
    ]

    barrier = pltpu.get_barrier_semaphore()
    each(1, cols, lambda k: pl.semaphore_signal(
        barrier, inc=1, device_id=along(k), device_id_type=MESH))
    each(1, rows, lambda k: pl.semaphore_signal(
        barrier, inc=1, device_id=across(k), device_id_type=MESH))
    for copy in mine_in:
        copy.start()
    for copy in mine_in[0:3]:
        copy.wait()
    row_all[my_col, :, 0:width] = pts_ref[0:rhs]
    row_all[my_col, :, width:2 * width] = pts_ref[rhs:dims]
    row_all[my_col, :, 2 * width:] = dir_ref[...]
    col_all[my_row, :, 0:width] = pts_ref[0:rhs]
    col_all[my_row, :, width:2 * width] = pts_ref[rhs:dims]
    col_all[my_row, :, 2 * width:3 * width] = dir_ref[...]
    col_all[my_row, :, 3 * width:] = res_ref[...]
    pl.semaphore_wait(barrier, cols - 1 + rows - 1)

    def share(ref, slot, send_sem, recv_sem, peer):
        pltpu.make_async_remote_copy(
            src_ref=ref.at[slot], dst_ref=ref.at[slot], send_sem=send_sem, recv_sem=recv_sem,
            device_id=peer, device_id_type=MESH).start()

    def wait_bytes(ref, sem):
        count = ref.shape[0] - 1
        pltpu.make_async_copy(ref.at[pl.ds(0, count)], ref.at[pl.ds(0, count)], sem).wait()

    each(1, rows, lambda k: share(col_all, my_row, col_send, col_recv, across(k)))
    each(1, cols, lambda k: share(row_all, my_col, row_send, row_recv.at[k], along(k)))

    for copy in mine_in[3:]:
        copy.wait()
    row = lax.broadcasted_iota(jnp.int32, (dims, width), 0)
    scale = jnp.zeros((dims, width), F32)
    for i in range(dims):
        scale = jnp.where(row == i, len_ref[i], scale)
    scale = STEP / scale

    def points_of(block):
        return jnp.concatenate([block[:, 0:width], block[:, width:2 * width]], axis=0) * scale

    wait_bytes(col_all, col_recv)
    right = jnp.concatenate([right_rows(points_of(col_all[j])) for j in range(rows)], axis=1).astype(BF16)

    tiles = max(1, right.shape[1] // TILE)
    totals = [jnp.zeros((4 * rhs, right.shape[1] // tiles), F32)] * tiles
    pair = math.gcd(cols, 2)
    for first in range(0, cols, pair):
        left, dirs = [], []
        for k in range(first, first + pair):
            source = partner(k)[1]
            if k > 0:
                pltpu.make_async_copy(row_all.at[source], row_all.at[source], row_recv.at[k]).wait()
            block = row_all[source]
            left.append(left_rows(points_of(block)))
            dirs.append(block[:, 2 * width:3 * width])
        left = jnp.concatenate(left, axis=1).T.astype(BF16)
        d1, d2, d3 = split3(jnp.concatenate(dirs, axis=1))
        dirs = jnp.concatenate([d1, d2, d3, jnp.zeros_like(d1)], axis=0).astype(BF16)
        totals = add_block(totals, left, right, dirs)
    part = jnp.concatenate([t[0:rhs] + t[rhs:2 * rhs] + t[2 * rhs:3 * rhs] for t in totals], axis=1)
    parts[my_row] = part
    each(1, rows, lambda k: share(parts, my_row, part_send, part_recv, across(k)))

    def over(x):
        return jnp.sum(x, axis=1, keepdims=True)

    direction = jnp.concatenate([col_all[j, :, 2 * width:3 * width] for j in range(rows)], axis=1)
    residual = jnp.concatenate([col_all[j, :, 3 * width:] for j in range(rows)], axis=1)
    rr = over(residual * residual)
    wait_bytes(parts, part_recv)
    image = sig_ref[0, 0] * jnp.sum(parts[...], axis=0) + noise_ref[0, 0] * direction

    dq, rq, qq = over(direction * image), over(residual * image), over(image * image)
    fits = qq > 1e-30
    near = jnp.where(fits, rq / jnp.where(fits, qq, 1.0), 0.0)
    left_over = residual - near * image
    pq, pp = over(left_over * image), over(left_over * left_over)
    lane = lax.broadcasted_iota(jnp.int32, (rhs, width), 1)
    mine = jnp.zeros((rhs, width), F32)
    for i, item in enumerate((dq, rr, near, qq, pq, pp)):
        mine = jnp.where(lane == i, item, mine)
    sums[my_col] = mine
    each(1, cols, lambda k: share(sums, my_col, sum_send, sum_recv, along(k)))

    for j in range(rows):
        images[j] = image[:, j * width:(j + 1) * width]
    wait_bytes(row_all, row_send)
    wait_bytes(col_all, col_send)
    wait_bytes(parts, part_send)
    wait_bytes(sums, sum_recv)

    def total_of(x):
        out = x[0:rhs]
        for j in range(1, cols):
            out = out + x[j * rhs:(j + 1) * rhs]
        return out

    every = jnp.concatenate([sums[j] for j in range(cols)], axis=0)

    def item(i):
        return every if i == 0 else pltpu.roll(every, width - i, 1)

    used = lane == 0
    all_rr = jnp.where(used, total_of(item(1)), 1.0)
    alpha = all_rr / jnp.where(used, total_of(every), 1.0)
    off = jnp.concatenate([alpha] * cols, axis=0) - item(2)
    new_rr = total_of(item(5) + off * (off * item(3) - 2.0 * item(4)))
    beta = new_rr / all_rr
    alpha, beta = alpha[:, 0:1], beta[:, 0:1]
    move_ref[0] = alpha * dir_ref[...]
    move_ref[1] = alpha * images[my_row]
    move_ref[2] = beta * dir_ref[...]
    wait_bytes(sums, sum_send)


def solution(mesh):
    rows, cols = mesh.shape["row"], mesh.shape["col"]

    def on_device(points, lengthscale, signal_var, noise_var, solution, residual, direction):
        rhs, width = direction.shape
        dims = points.shape[0]
        vmem = pl.BlockSpec(memory_space=pltpu.VMEM)
        hbm = pl.BlockSpec(memory_space=pltpu.HBM)
        move = pl.pallas_call(
            functools.partial(cg_kernel, rows, cols),
            out_shape=jax.ShapeDtypeStruct((3, rhs, width), F32),
            in_specs=[hbm] * 6,
            out_specs=vmem,
            scratch_shapes=[
                pltpu.SMEM((dims,), F32),
                pltpu.SMEM((1, 1), F32),
                pltpu.SMEM((1, 1), F32),
                pltpu.VMEM((dims, width), F32),
                pltpu.VMEM((rhs, width), F32),
                pltpu.VMEM((rhs, width), F32),
                pltpu.VMEM((cols, rhs, 3 * width), F32),
                pltpu.VMEM((rows, rhs, 4 * width), F32),
                pltpu.VMEM((rows, rhs, rows * width), F32),
                pltpu.VMEM((rows, rhs, width), F32),
                pltpu.VMEM((cols, rhs, width), F32),
                pltpu.SemaphoreType.DMA((6,)),
                pltpu.SemaphoreType.DMA,
                pltpu.SemaphoreType.DMA((cols,)),
            ] + [pltpu.SemaphoreType.DMA] * 6,
            compiler_params=pltpu.CompilerParams(
                collective_id=0, has_side_effects=True, vmem_limit_bytes=60 * 1024 * 1024),
            cost_estimate=pl.CostEstimate(
                flops=2 * 80 * rows * cols * width * width, bytes_accessed=32 * 1024,
                transcendentals=2 * rows * cols * width * width),
        )(lengthscale, signal_var.reshape(1, 1), noise_var.reshape(1, 1), points, residual, direction)
        new_residual = residual - move[1]
        return solution + move[0], new_residual, new_residual + move[2]

    spread = P(None, ("row", "col"))
    return jax.shard_map(
        on_device, mesh=mesh, in_specs=(spread, P(), P(), P(), spread, spread, spread),
        out_specs=(spread, spread, spread), check_vma=False)
```

```python
import functools
import math

import jax
import jax.numpy as jnp
from jax import lax
from jax.experimental import pallas as pl
from jax.experimental.pallas import tpu as pltpu
from jax.sharding import PartitionSpec as P

MESH = pl.DeviceIdType.MESH
F32 = jnp.float32
BF16 = jnp.bfloat16
STEP = math.sqrt(5.0)
TILE = 256


def split3(x):
    a = x.astype(BF16).astype(F32)
    rest = x - a
    b = rest.astype(BF16).astype(F32)
    c = (rest - b).astype(BF16).astype(F32)
    return a, b, c


def norm_rows(x, first):
    n1, n2, n3 = split3(jnp.sum(x * x, axis=0, keepdims=True))
    row = lax.broadcasted_iota(jnp.int32, x.shape, 0)
    base = 0 if first else 3
    ones = (row >= 3 - base) & (row < 6 - base)
    out = jnp.where(ones, 1.0, 0.0)
    for i, part in enumerate((n1, n2, n3)):
        out = jnp.where(row == base + i, part, out)
    return out


def left_rows(x):
    a, b, c = split3(x)
    rows = [-2.0 * v for v in (a, a, b, b, a, c)]
    return jnp.concatenate(rows + [norm_rows(x, False), jnp.zeros_like(x)], axis=0)


def right_rows(x):
    a, b, c = split3(x)
    return jnp.concatenate([a, b, a, b, c, a, norm_rows(x, True), jnp.zeros_like(x)], axis=0)


def each(low, high, body):
    for k in range(low, high):
        body(k)


def add_block(totals, left, right, dirs):
    deep, wide = min(128, left.shape[0]), right.shape[1] // len(totals)
    out = []
    for j, total in enumerate(totals):
        for i in range(0, left.shape[0], deep):
            v = jnp.dot(left[i:i + deep], right[:, j * wide:(j + 1) * wide], preferred_element_type=F32)
            v = jnp.maximum(v, 1e-30)
            t = v * lax.rsqrt(v)
            kern = (1.0 + t + (1.0 / 3.0) * v) * jnp.exp(-t)
            k1 = kern.astype(BF16)
            k2 = (kern - k1.astype(F32)).astype(BF16)
            rows = dirs[:, i:i + deep]
            total += jnp.dot(rows, k1, preferred_element_type=F32)
            total += jnp.dot(rows, k2, preferred_element_type=F32)
        out.append(total)
    return out


def cg_kernel(rows, cols, len_hbm, sig_hbm, noise_hbm, pts_ref, res_ref, dir_ref, move_ref,
              len_ref, sig_ref, noise_ref, row_all, col_all, parts, images, sums, in_sem,
              row_send, row_recv, col_send, col_recv, part_send, part_recv, sum_send, sum_recv):
    my_row, my_col = lax.axis_index("row"), lax.axis_index("col")
    dims, width = pts_ref.shape
    rhs = res_ref.shape[0]

    def partner(k):
        if cols & (cols - 1):
            return lax.rem(my_col + k, cols), lax.rem(my_col + cols - k, cols)
        peer = my_col
        for b in range(cols.bit_length()):
            if (k >> b) & 1:
                peer = peer + (1 << b) - (2 << b) * lax.rem(my_col // (1 << b), 2)
        return peer, peer

    def along(k):
        return (my_row, partner(k)[0])

    def across(k):
        return (lax.rem(my_row + k, rows), my_col)

    mine_in = [
        pltpu.make_async_copy(len_hbm, len_ref, in_sem.at[0]),
        pltpu.make_async_copy(sig_hbm, sig_ref, in_sem.at[1]),
        pltpu.make_async_copy(noise_hbm, noise_ref, in_sem.at[2]),
    ]

    barrier = pltpu.get_barrier_semaphore()
    each(1, cols, lambda k: pl.semaphore_signal(
        barrier, inc=1, device_id=along(k), device_id_type=MESH))
    each(1, rows, lambda k: pl.semaphore_signal(
        barrier, inc=1, device_id=across(k), device_id_type=MESH))
    for copy in mine_in:
        copy.start()
    row_all[my_col, :, 0:width] = pts_ref[0:rhs]
    row_all[my_col, :, width:2 * width] = pts_ref[rhs:dims]
    row_all[my_col, :, 2 * width:] = dir_ref[...]
    col_all[my_row, :, 0:width] = pts_ref[0:rhs]
    col_all[my_row, :, width:2 * width] = pts_ref[rhs:dims]
    col_all[my_row, :, 2 * width:3 * width] = dir_ref[...]
    col_all[my_row, :, 3 * width:] = res_ref[...]
    pl.semaphore_wait(barrier, cols - 1 + rows - 1)

    def share(ref, slot, send_sem, recv_sem, peer):
        pltpu.make_async_remote_copy(
            src_ref=ref.at[slot], dst_ref=ref.at[slot], send_sem=send_sem, recv_sem=recv_sem,
            device_id=peer, device_id_type=MESH).start()

    def wait_bytes(ref, sem):
        count = ref.shape[0] - 1
        pltpu.make_async_copy(ref.at[pl.ds(0, count)], ref.at[pl.ds(0, count)], sem).wait()

    each(1, rows, lambda k: share(col_all, my_row, col_send, col_recv, across(k)))
    each(1, cols, lambda k: share(row_all, my_col, row_send, row_recv.at[k], along(k)))

    for copy in mine_in:
        copy.wait()
    row = lax.broadcasted_iota(jnp.int32, (dims, width), 0)
    scale = jnp.zeros((dims, width), F32)
    for i in range(dims):
        scale = jnp.where(row == i, len_ref[i], scale)
    scale = STEP / scale

    def points_of(block):
        return jnp.concatenate([block[:, 0:width], block[:, width:2 * width]], axis=0) * scale

    wait_bytes(col_all, col_recv)
    right = jnp.concatenate([right_rows(points_of(col_all[j])) for j in range(rows)], axis=1).astype(BF16)

    tiles = max(1, right.shape[1] // TILE)
    totals = [jnp.zeros((4 * rhs, right.shape[1] // tiles), F32)] * tiles
    pair = math.gcd(cols, 2)
    for first in range(0, cols, pair):
        left, dirs = [], []
        for k in range(first, first + pair):
            source = partner(k)[1]
            if k > 0:
                pltpu.make_async_copy(row_all.at[source], row_all.at[source], row_recv.at[k]).wait()
            block = row_all[source]
            left.append(left_rows(points_of(block)))
            dirs.append(block[:, 2 * width:3 * width])
        left = jnp.concatenate(left, axis=1).T.astype(BF16)
        d1, d2, d3 = split3(jnp.concatenate(dirs, axis=1))
        dirs = jnp.concatenate([d1, d2, d3, jnp.zeros_like(d1)], axis=0).astype(BF16)
        totals = add_block(totals, left, right, dirs)
    part = jnp.concatenate([t[0:rhs] + t[rhs:2 * rhs] + t[2 * rhs:3 * rhs] for t in totals], axis=1)
    parts[my_row] = part
    each(1, rows, lambda k: share(parts, my_row, part_send, part_recv, across(k)))

    def over(x):
        return jnp.sum(x, axis=1, keepdims=True)

    direction = jnp.concatenate([col_all[j, :, 2 * width:3 * width] for j in range(rows)], axis=1)
    residual = jnp.concatenate([col_all[j, :, 3 * width:] for j in range(rows)], axis=1)
    rr = over(residual * residual)
    wait_bytes(parts, part_recv)
    image = sig_ref[0, 0] * jnp.sum(parts[...], axis=0) + noise_ref[0, 0] * direction

    dq, rq, qq = over(direction * image), over(residual * image), over(image * image)
    fits = qq > 1e-30
    near = jnp.where(fits, rq / jnp.where(fits, qq, 1.0), 0.0)
    left_over = residual - near * image
    pq, pp = over(left_over * image), over(left_over * left_over)
    lane = lax.broadcasted_iota(jnp.int32, (rhs, width), 1)
    mine = jnp.zeros((rhs, width), F32)
    for i, item in enumerate((dq, rr, near, qq, pq, pp)):
        mine = jnp.where(lane == i, item, mine)
    sums[my_col] = mine
    each(1, cols, lambda k: share(sums, my_col, sum_send, sum_recv, along(k)))

    for j in range(rows):
        images[j] = image[:, j * width:(j + 1) * width]
    wait_bytes(row_all, row_send)
    wait_bytes(col_all, col_send)
    wait_bytes(parts, part_send)
    wait_bytes(sums, sum_recv)

    def total_of(x):
        out = x[0:rhs]
        for j in range(1, cols):
            out = out + x[j * rhs:(j + 1) * rhs]
        return out

    every = jnp.concatenate([sums[j] for j in range(cols)], axis=0)

    def item(i):
        return every if i == 0 else pltpu.roll(every, width - i, 1)

    used = lane == 0
    all_rr = jnp.where(used, total_of(item(1)), 1.0)
    alpha = all_rr / jnp.where(used, total_of(every), 1.0)
    off = jnp.concatenate([alpha] * cols, axis=0) - item(2)
    new_rr = total_of(item(5) + off * (off * item(3) - 2.0 * item(4)))
    beta = new_rr / all_rr
    alpha, beta = alpha[:, 0:1], beta[:, 0:1]
    move_ref[0] = alpha * dir_ref[...]
    move_ref[1] = alpha * images[my_row]
    move_ref[2] = beta * dir_ref[...]
    wait_bytes(sums, sum_send)


def solution(mesh):
    rows, cols = mesh.shape["row"], mesh.shape["col"]

    def on_device(points, lengthscale, signal_var, noise_var, solution, residual, direction):
        rhs, width = direction.shape
        dims = points.shape[0]
        vmem = pl.BlockSpec(memory_space=pltpu.VMEM)
        hbm = pl.BlockSpec(memory_space=pltpu.HBM)
        move = pl.pallas_call(
            functools.partial(cg_kernel, rows, cols),
            out_shape=jax.ShapeDtypeStruct((3, rhs, width), F32),
            in_specs=[hbm] * 3 + [vmem] * 3,
            out_specs=vmem,
            scratch_shapes=[
                pltpu.SMEM((dims,), F32),
                pltpu.SMEM((1, 1), F32),
                pltpu.SMEM((1, 1), F32),
                pltpu.VMEM((cols, rhs, 3 * width), F32),
                pltpu.VMEM((rows, rhs, 4 * width), F32),
                pltpu.VMEM((rows, rhs, rows * width), F32),
                pltpu.VMEM((rows, rhs, width), F32),
                pltpu.VMEM((cols, rhs, width), F32),
                pltpu.SemaphoreType.DMA((3,)),
                pltpu.SemaphoreType.DMA,
                pltpu.SemaphoreType.DMA((cols,)),
            ] + [pltpu.SemaphoreType.DMA] * 6,
            compiler_params=pltpu.CompilerParams(
                collective_id=0, has_side_effects=True, vmem_limit_bytes=32 * 1024 * 1024),
            cost_estimate=pl.CostEstimate(
                flops=2 * 80 * rows * cols * width * width, bytes_accessed=32 * 1024,
                transcendentals=2 * rows * cols * width * width),
        )(lengthscale, signal_var.reshape(1, 1), noise_var.reshape(1, 1), points, residual, direction)
        new_residual = residual - move[1]
        return solution + move[0], new_residual, new_residual + move[2]

    spread = P(None, ("row", "col"))
    return jax.shard_map(
        on_device, mesh=mesh, in_specs=(spread, P(), P(), P(), spread, spread, spread),
        out_specs=(spread, spread, spread), check_vma=False)
```

```python
import functools
import math

import jax
import jax.numpy as jnp
from jax import lax
from jax.experimental import pallas as pl
from jax.experimental.pallas import tpu as pltpu
from jax.sharding import PartitionSpec as P

MESH = pl.DeviceIdType.MESH
F32 = jnp.float32
BF16 = jnp.bfloat16
STEP = math.sqrt(5.0)
TILE = 256


def split3(x):
    a = x.astype(BF16).astype(F32)
    rest = x - a
    b = rest.astype(BF16).astype(F32)
    c = (rest - b).astype(BF16).astype(F32)
    return a, b, c


def norm_rows(x, first):
    n1, n2, n3 = split3(jnp.sum(x * x, axis=0, keepdims=True))
    row = lax.broadcasted_iota(jnp.int32, x.shape, 0)
    base = 0 if first else 3
    ones = (row >= 3 - base) & (row < 6 - base)
    out = jnp.where(ones, 1.0, 0.0)
    for i, part in enumerate((n1, n2, n3)):
        out = jnp.where(row == base + i, part, out)
    return out


def left_rows(x):
    a, b, c = split3(x)
    rows = [-2.0 * v for v in (a, a, b, b, a, c)]
    return jnp.concatenate(rows + [norm_rows(x, False), jnp.zeros_like(x)], axis=0)


def right_rows(x):
    a, b, c = split3(x)
    return jnp.concatenate([a, b, a, b, c, a, norm_rows(x, True), jnp.zeros_like(x)], axis=0)


def each(low, high, body):
    for k in range(low, high):
        body(k)


def add_block(totals, left, right, dirs):
    deep, wide = min(128, left.shape[0]), right.shape[1] // len(totals)
    out = []
    for j, total in enumerate(totals):
        for i in range(0, left.shape[0], deep):
            v = jnp.dot(left[i:i + deep], right[:, j * wide:(j + 1) * wide], preferred_element_type=F32)
            v = jnp.maximum(v, 1e-30)
            t = v * lax.rsqrt(v)
            kern = (1.0 + t + (1.0 / 3.0) * v) * jnp.exp(-t)
            k1 = kern.astype(BF16)
            k2 = (kern - k1.astype(F32)).astype(BF16)
            rows = dirs[:, i:i + deep]
            total += jnp.dot(rows, k1, preferred_element_type=F32)
            total += jnp.dot(rows, k2, preferred_element_type=F32)
        out.append(total)
    return out


def cg_kernel(rows, cols, len_hbm, sig_hbm, noise_hbm, pts_ref, res_ref, dir_ref, move_ref,
              len_ref, sig_ref, noise_ref, row_all, col_all, parts, images, sums, in_sem,
              row_send, row_recv, col_send, col_recv, part_send, part_recv, sum_send, sum_recv):
    my_row, my_col = lax.axis_index("row"), lax.axis_index("col")
    dims, width = pts_ref.shape
    rhs = res_ref.shape[0]

    def partner(k):
        if cols & (cols - 1):
            return lax.rem(my_col + k, cols), lax.rem(my_col + cols - k, cols)
        peer = my_col
        for b in range(cols.bit_length()):
            if (k >> b) & 1:
                peer = peer + (1 << b) - (2 << b) * lax.rem(my_col // (1 << b), 2)
        return peer, peer

    def along(k):
        return (my_row, partner(k)[0])

    def across(k):
        return (lax.rem(my_row + k, rows), my_col)

    mine_in = [
        pltpu.make_async_copy(len_hbm, len_ref, in_sem.at[0]),
        pltpu.make_async_copy(sig_hbm, sig_ref, in_sem.at[1]),
        pltpu.make_async_copy(noise_hbm, noise_ref, in_sem.at[2]),
    ]

    barrier = pltpu.get_barrier_semaphore()
    each(1, cols, lambda k: pl.semaphore_signal(
        barrier, inc=1, device_id=along(k), device_id_type=MESH))
    each(1, rows, lambda k: pl.semaphore_signal(
        barrier, inc=1, device_id=across(k), device_id_type=MESH))
    for copy in mine_in:
        copy.start()
    row_all[my_col, :, 0:width] = pts_ref[0:rhs]
    row_all[my_col, :, width:2 * width] = pts_ref[rhs:dims]
    row_all[my_col, :, 2 * width:] = dir_ref[...]
    col_all[my_row, :, 0:width] = pts_ref[0:rhs]
    col_all[my_row, :, width:2 * width] = pts_ref[rhs:dims]
    col_all[my_row, :, 2 * width:3 * width] = dir_ref[...]
    col_all[my_row, :, 3 * width:] = res_ref[...]
    pl.semaphore_wait(barrier, cols - 1 + rows - 1)

    def share(ref, slot, send_sem, recv_sem, peer):
        pltpu.make_async_remote_copy(
            src_ref=ref.at[slot], dst_ref=ref.at[slot], send_sem=send_sem, recv_sem=recv_sem,
            device_id=peer, device_id_type=MESH).start()

    def wait_bytes(ref, sem):
        count = ref.shape[0] - 1
        pltpu.make_async_copy(ref.at[pl.ds(0, count)], ref.at[pl.ds(0, count)], sem).wait()

    each(1, rows, lambda k: share(col_all, my_row, col_send, col_recv, across(k)))
    each(1, cols, lambda k: share(row_all, my_col, row_send, row_recv.at[k], along(k)))

    for copy in mine_in:
        copy.wait()
    row = lax.broadcasted_iota(jnp.int32, (dims, width), 0)
    scale = jnp.zeros((dims, width), F32)
    for i in range(dims):
        scale = jnp.where(row == i, len_ref[0, i], scale)
    scale = STEP / scale

    def points_of(block):
        return jnp.concatenate([block[:, 0:width], block[:, width:2 * width]], axis=0) * scale

    wait_bytes(col_all, col_recv)
    right = jnp.concatenate([right_rows(points_of(col_all[j])) for j in range(rows)], axis=1).astype(BF16)

    tiles = max(1, right.shape[1] // TILE)
    totals = [jnp.zeros((4 * rhs, right.shape[1] // tiles), F32)] * tiles
    pair = math.gcd(cols, 2)
    for first in range(0, cols, pair):
        left, dirs = [], []
        for k in range(first, first + pair):
            source = partner(k)[1]
            if k > 0:
                pltpu.make_async_copy(row_all.at[source], row_all.at[source], row_recv.at[k]).wait()
            block = row_all[source]
            left.append(left_rows(points_of(block)))
            dirs.append(block[:, 2 * width:3 * width])
        left = jnp.concatenate(left, axis=1).T.astype(BF16)
        d1, d2, d3 = split3(jnp.concatenate(dirs, axis=1))
        dirs = jnp.concatenate([d1, d2, d3, jnp.zeros_like(d1)], axis=0).astype(BF16)
        totals = add_block(totals, left, right, dirs)
    part = jnp.concatenate([t[0:rhs] + t[rhs:2 * rhs] + t[2 * rhs:3 * rhs] for t in totals], axis=1)
    parts[my_row] = part
    each(1, rows, lambda k: share(parts, my_row, part_send, part_recv, across(k)))

    def over(x):
        return jnp.sum(x, axis=1, keepdims=True)

    direction = jnp.concatenate([col_all[j, :, 2 * width:3 * width] for j in range(rows)], axis=1)
    residual = jnp.concatenate([col_all[j, :, 3 * width:] for j in range(rows)], axis=1)
    rr = over(residual * residual)
    wait_bytes(parts, part_recv)
    image = sig_ref[0, 0] * jnp.sum(parts[...], axis=0) + noise_ref[0, 0] * direction

    dq, rq, qq = over(direction * image), over(residual * image), over(image * image)
    fits = qq > 1e-30
    near = jnp.where(fits, rq / jnp.where(fits, qq, 1.0), 0.0)
    left_over = residual - near * image
    pq, pp = over(left_over * image), over(left_over * left_over)
    lane = lax.broadcasted_iota(jnp.int32, (rhs, width), 1)
    mine = jnp.zeros((rhs, width), F32)
    for i, item in enumerate((dq, rr, near, qq, pq, pp)):
        mine = jnp.where(lane == i, item, mine)
    sums[my_col] = mine
    each(1, cols, lambda k: share(sums, my_col, sum_send, sum_recv, along(k)))

    for j in range(rows):
        images[j] = image[:, j * width:(j + 1) * width]
    wait_bytes(row_all, row_send)
    wait_bytes(col_all, col_send)
    wait_bytes(parts, part_send)
    wait_bytes(sums, sum_recv)

    def total_of(x):
        out = x[0:rhs]
        for j in range(1, cols):
            out = out + x[j * rhs:(j + 1) * rhs]
        return out

    every = jnp.concatenate([sums[j] for j in range(cols)], axis=0)

    def item(i):
        return every if i == 0 else pltpu.roll(every, width - i, 1)

    used = lane == 0
    all_rr = jnp.where(used, total_of(item(1)), 1.0)
    alpha = all_rr / jnp.where(used, total_of(every), 1.0)
    off = jnp.concatenate([alpha] * cols, axis=0) - item(2)
    new_rr = total_of(item(5) + off * (off * item(3) - 2.0 * item(4)))
    beta = new_rr / all_rr
    alpha, beta = alpha[:, 0:1], beta[:, 0:1]
    move_ref[0] = alpha * dir_ref[...]
    move_ref[1] = alpha * images[my_row]
    move_ref[2] = beta * dir_ref[...]
    wait_bytes(sums, sum_send)


def solution(mesh):
    rows, cols = mesh.shape["row"], mesh.shape["col"]

    def on_device(points, lengthscale, signal_var, noise_var, solution, residual, direction):
        rhs, width = direction.shape
        dims = points.shape[0]
        vmem = pl.BlockSpec(memory_space=pltpu.VMEM)
        hbm = pl.BlockSpec(memory_space=pltpu.HBM)
        move = pl.pallas_call(
            functools.partial(cg_kernel, rows, cols),
            out_shape=jax.ShapeDtypeStruct((3, rhs, width), F32),
            in_specs=[hbm] * 3 + [vmem] * 3,
            out_specs=vmem,
            scratch_shapes=[
                pltpu.SMEM((1, dims), F32),
                pltpu.SMEM((1, 1), F32),
                pltpu.SMEM((1, 1), F32),
                pltpu.VMEM((cols, rhs, 3 * width), F32),
                pltpu.VMEM((rows, rhs, 4 * width), F32),
                pltpu.VMEM((rows, rhs, rows * width), F32),
                pltpu.VMEM((rows, rhs, width), F32),
                pltpu.VMEM((cols, rhs, width), F32),
                pltpu.SemaphoreType.DMA((3,)),
                pltpu.SemaphoreType.DMA,
                pltpu.SemaphoreType.DMA((cols,)),
            ] + [pltpu.SemaphoreType.DMA] * 6,
            compiler_params=pltpu.CompilerParams(
                collective_id=0, has_side_effects=True, vmem_limit_bytes=32 * 1024 * 1024),
            cost_estimate=pl.CostEstimate(
                flops=2 * 80 * rows * cols * width * width, bytes_accessed=32 * 1024,
                transcendentals=2 * rows * cols * width * width),
        )(lengthscale.reshape(1, -1), signal_var.reshape(1, 1), noise_var.reshape(1, 1), points, residual, direction)
        new_residual = residual - move[1]
        return solution + move[0], new_residual, new_residual + move[2]

    spread = P(None, ("row", "col"))
    return jax.shard_map(
        on_device, mesh=mesh, in_specs=(spread, P(), P(), P(), spread, spread, spread),
        out_specs=(spread, spread, spread), check_vma=False)
```

```python
import functools
import math

import jax
import jax.numpy as jnp
from jax import lax
from jax.experimental import pallas as pl
from jax.experimental.pallas import tpu as pltpu
from jax.sharding import PartitionSpec as P

MESH = pl.DeviceIdType.MESH
F32 = jnp.float32
BF16 = jnp.bfloat16
STEP = math.sqrt(5.0)
TILE = 256


def split3(x):
    a = x.astype(BF16).astype(F32)
    rest = x - a
    b = rest.astype(BF16).astype(F32)
    c = (rest - b).astype(BF16).astype(F32)
    return a, b, c


def norm_rows(x, first):
    n1, n2, n3 = split3(jnp.sum(x * x, axis=0, keepdims=True))
    row = lax.broadcasted_iota(jnp.int32, x.shape, 0)
    base = 0 if first else 3
    ones = (row >= 3 - base) & (row < 6 - base)
    out = jnp.where(ones, 1.0, 0.0)
    for i, part in enumerate((n1, n2, n3)):
        out = jnp.where(row == base + i, part, out)
    return out


def left_rows(x):
    a, b, c = split3(x)
    rows = [-2.0 * v for v in (a, a, b, b, a, c)]
    return jnp.concatenate(rows + [norm_rows(x, False), jnp.zeros_like(x)], axis=0)


def right_rows(x):
    a, b, c = split3(x)
    return jnp.concatenate([a, b, a, b, c, a, norm_rows(x, True), jnp.zeros_like(x)], axis=0)


def each(low, high, body):
    for k in range(low, high):
        body(k)


def add_block(totals, left, right, dirs):
    deep, wide = min(128, left.shape[0]), right.shape[1] // len(totals)
    out = []
    for j, total in enumerate(totals):
        for i in range(0, left.shape[0], deep):
            v = jnp.dot(left[i:i + deep], right[:, j * wide:(j + 1) * wide], preferred_element_type=F32)
            v = jnp.maximum(v, 1e-30)
            t = v * lax.rsqrt(v)
            kern = (1.0 + t + (1.0 / 3.0) * v) * jnp.exp(-t)
            k1 = kern.astype(BF16)
            k2 = (kern - k1.astype(F32)).astype(BF16)
            rows = dirs[:, i:i + deep]
            total += jnp.dot(rows, k1, preferred_element_type=F32)
            total += jnp.dot(rows, k2, preferred_element_type=F32)
        out.append(total)
    return out


def cg_kernel(rows, cols, len_hbm, sig_hbm, noise_hbm, pts_ref, res_ref, dir_ref, move_ref,
              len_ref, sig_ref, noise_ref, row_all, col_all, parts, images, sums, in_sem,
              row_send, row_recv, col_send, col_recv, part_send, part_recv, sum_send, sum_recv):
    my_row, my_col = lax.axis_index("row"), lax.axis_index("col")
    dims, width = pts_ref.shape
    rhs = res_ref.shape[0]

    def partner(k):
        if cols & (cols - 1):
            return lax.rem(my_col + k, cols), lax.rem(my_col + cols - k, cols)
        peer = my_col
        for b in range(cols.bit_length()):
            if (k >> b) & 1:
                peer = peer + (1 << b) - (2 << b) * lax.rem(my_col // (1 << b), 2)
        return peer, peer

    def along(k):
        return (my_row, partner(k)[0])

    def across(k):
        return (lax.rem(my_row + k, rows), my_col)

    mine_in = [
        pltpu.make_async_copy(len_hbm, len_ref, in_sem.at[0]),
        pltpu.make_async_copy(sig_hbm, sig_ref, in_sem.at[1]),
        pltpu.make_async_copy(noise_hbm, noise_ref, in_sem.at[2]),
    ]

    barrier = pltpu.get_barrier_semaphore()
    each(1, cols, lambda k: pl.semaphore_signal(
        barrier, inc=1, device_id=along(k), device_id_type=MESH))
    each(1, rows, lambda k: pl.semaphore_signal(
        barrier, inc=1, device_id=across(k), device_id_type=MESH))
    for copy in mine_in:
        copy.start()
    row_all[my_col, :, 0:width] = pts_ref[0:rhs]
    row_all[my_col, :, width:2 * width] = pts_ref[rhs:dims]
    row_all[my_col, :, 2 * width:] = dir_ref[...]
    col_all[my_row, :, 0:width] = pts_ref[0:rhs]
    col_all[my_row, :, width:2 * width] = pts_ref[rhs:dims]
    col_all[my_row, :, 2 * width:3 * width] = dir_ref[...]
    col_all[my_row, :, 3 * width:] = res_ref[...]
    pl.semaphore_wait(barrier, cols - 1 + rows - 1)

    def share(ref, slot, send_sem, recv_sem, peer):
        pltpu.make_async_remote_copy(
            src_ref=ref.at[slot], dst_ref=ref.at[slot], send_sem=send_sem, recv_sem=recv_sem,
            device_id=peer, device_id_type=MESH).start()

    def wait_bytes(ref, sem):
        count = ref.shape[0] - 1
        pltpu.make_async_copy(ref.at[pl.ds(0, count)], ref.at[pl.ds(0, count)], sem).wait()

    each(1, rows, lambda k: share(col_all, my_row, col_send, col_recv, across(k)))
    each(1, cols, lambda k: share(row_all, my_col, row_send, row_recv.at[cols - k], along(cols - k)))

    for copy in mine_in:
        copy.wait()
    row = lax.broadcasted_iota(jnp.int32, (dims, width), 0)
    scale = jnp.zeros((dims, width), F32)
    for i in range(dims):
        scale = jnp.where(row == i, len_ref[0, i], scale)
    scale = STEP / scale

    def points_of(block):
        return jnp.concatenate([block[:, 0:width], block[:, width:2 * width]], axis=0) * scale

    wait_bytes(col_all, col_recv)
    right = jnp.concatenate([right_rows(points_of(col_all[j])) for j in range(rows)], axis=1).astype(BF16)

    tiles = max(1, right.shape[1] // TILE)
    totals = [jnp.zeros((4 * rhs, right.shape[1] // tiles), F32)] * tiles
    pair = math.gcd(cols, 4)
    for first in range(0, cols, pair):
        left, dirs = [], []
        for k in range(first, first + pair):
            source = partner(k)[1]
            if k > 0:
                pltpu.make_async_copy(row_all.at[source], row_all.at[source], row_recv.at[k]).wait()
            block = row_all[source]
            left.append(left_rows(points_of(block)))
            dirs.append(block[:, 2 * width:3 * width])
        left = jnp.concatenate(left, axis=1).T.astype(BF16)
        d1, d2, d3 = split3(jnp.concatenate(dirs, axis=1))
        dirs = jnp.concatenate([d1, d2, d3, jnp.zeros_like(d1)], axis=0).astype(BF16)
        totals = add_block(totals, left, right, dirs)
    part = jnp.concatenate([t[0:rhs] + t[rhs:2 * rhs] + t[2 * rhs:3 * rhs] for t in totals], axis=1)
    parts[my_row] = part
    each(1, rows, lambda k: share(parts, my_row, part_send, part_recv, across(k)))

    def over(x):
        return jnp.sum(x, axis=1, keepdims=True)

    direction = jnp.concatenate([col_all[j, :, 2 * width:3 * width] for j in range(rows)], axis=1)
    residual = jnp.concatenate([col_all[j, :, 3 * width:] for j in range(rows)], axis=1)
    rr = over(residual * residual)
    wait_bytes(parts, part_recv)
    image = sig_ref[0, 0] * jnp.sum(parts[...], axis=0) + noise_ref[0, 0] * direction

    dq, rq, qq = over(direction * image), over(residual * image), over(image * image)
    fits = qq > 1e-30
    near = jnp.where(fits, rq / jnp.where(fits, qq, 1.0), 0.0)
    left_over = residual - near * image
    pq, pp = over(left_over * image), over(left_over * left_over)
    lane = lax.broadcasted_iota(jnp.int32, (rhs, width), 1)
    mine = jnp.zeros((rhs, width), F32)
    for i, item in enumerate((dq, rr, near, qq, pq, pp)):
        mine = jnp.where(lane == i, item, mine)
    sums[my_col] = mine
    each(1, cols, lambda k: share(sums, my_col, sum_send, sum_recv, along(k)))

    for j in range(rows):
        images[j] = image[:, j * width:(j + 1) * width]
    wait_bytes(sums, sum_recv)

    def total_of(x):
        out = x[0:rhs]
        for j in range(1, cols):
            out = out + x[j * rhs:(j + 1) * rhs]
        return out

    every = jnp.concatenate([sums[j] for j in range(cols)], axis=0)

    def item(i):
        return every if i == 0 else pltpu.roll(every, width - i, 1)

    used = lane == 0
    all_rr = jnp.where(used, total_of(item(1)), 1.0)
    alpha = all_rr / jnp.where(used, total_of(every), 1.0)
    off = jnp.concatenate([alpha] * cols, axis=0) - item(2)
    new_rr = total_of(item(5) + off * (off * item(3) - 2.0 * item(4)))
    beta = new_rr / all_rr
    alpha, beta = alpha[:, 0:1], beta[:, 0:1]
    move_ref[0] = alpha * dir_ref[...]
    move_ref[1] = alpha * images[my_row]
    move_ref[2] = beta * dir_ref[...]
    wait_bytes(row_all, row_send)
    wait_bytes(col_all, col_send)
    wait_bytes(parts, part_send)
    wait_bytes(sums, sum_send)


def solution(mesh):
    rows, cols = mesh.shape["row"], mesh.shape["col"]

    def on_device(points, lengthscale, signal_var, noise_var, solution, residual, direction):
        rhs, width = direction.shape
        dims = points.shape[0]
        vmem = pl.BlockSpec(memory_space=pltpu.VMEM)
        hbm = pl.BlockSpec(memory_space=pltpu.HBM)
        move = pl.pallas_call(
            functools.partial(cg_kernel, rows, cols),
            out_shape=jax.ShapeDtypeStruct((3, rhs, width), F32),
            in_specs=[hbm] * 3 + [vmem] * 3,
            out_specs=vmem,
            scratch_shapes=[
                pltpu.SMEM((1, dims), F32),
                pltpu.SMEM((1, 1), F32),
                pltpu.SMEM((1, 1), F32),
                pltpu.VMEM((cols, rhs, 3 * width), F32),
                pltpu.VMEM((rows, rhs, 4 * width), F32),
                pltpu.VMEM((rows, rhs, rows * width), F32),
                pltpu.VMEM((rows, rhs, width), F32),
                pltpu.VMEM((cols, rhs, width), F32),
                pltpu.SemaphoreType.DMA((3,)),
                pltpu.SemaphoreType.DMA,
                pltpu.SemaphoreType.DMA((cols,)),
            ] + [pltpu.SemaphoreType.DMA] * 6,
            compiler_params=pltpu.CompilerParams(
                collective_id=0, has_side_effects=True, vmem_limit_bytes=32 * 1024 * 1024),
            cost_estimate=pl.CostEstimate(
                flops=2 * 80 * rows * cols * width * width, bytes_accessed=32 * 1024,
                transcendentals=2 * rows * cols * width * width),
        )(lengthscale.reshape(1, -1), signal_var.reshape(1, 1), noise_var.reshape(1, 1), points, residual, direction)
        new_residual = residual - move[1]
        return solution + move[0], new_residual, new_residual + move[2]

    spread = P(None, ("row", "col"))
    return jax.shard_map(
        on_device, mesh=mesh, in_specs=(spread, P(), P(), P(), spread, spread, spread),
        out_specs=(spread, spread, spread), check_vma=False)
```
